256 devices in a mesh: row: 8 (over y, core), col: 32 (over z, x).
Axes of the slice: x: 4, y: 4, z: 8, core: 2. Of those that a mesh axis runs over, the one named last changes fastest.
Arguments:
- kernel: float32 [8, 8, 256, 2, 32, 256], P(None, 'row', None, None, 'col'), may hold values from -40 to 40, as said below
Outputs:
- trailing: float32 [8, 8, 256, 2, 32, 256], P(None, 'row', None, None, 'col')
- panels: float32 [8, 8, 256, 3, 256], P(None, 'row')
The draws below stay inside these ranges and needn't reach their ends.
Inputs may be any that keep to these rules, and one draw needn't show every extreme that they name: kernel is symmetric and positive definite with smallest eigenvalue at least 1.
All inputs are finite; a program needn't handle non-finite values.
Results may differ from the reference program's by a relative error of at most 0.0003.
Values sent between devices are 32-bit elements; how exact they have to be, the bound alone decides.
No kernel may reach another device: no remote copies, remote signals or barrier semaphores. Data moves between devices by JAX's collectives and lax.ppermute only.
A program may use at most 128 MiB of HBM per device.

```python
import jax
import jax.numpy as jnp
from jax import lax

TILE = 256
FEATURES = 1024
STEPS = 3
COL_TILES = 2
TILES = 64
ROW_TILES = 8
ORDER = 16384


def draw_kernel(key, part):
    key_main = jax.random.fold_in(key, 11)
    features = jax.random.normal(key_main, (ORDER, FEATURES), jnp.float32)
    gram = jnp.dot(features, features.T, precision=lax.Precision.HIGHEST) / FEATURES
    gram = gram + jnp.eye(ORDER, dtype=jnp.float32)
    return gram.reshape(ROW_TILES, TILES // ROW_TILES, TILE, COL_TILES, TILES // COL_TILES, TILE)


def setup_inputs(seed: int = 0) -> dict:
    streams_of = jax.random.split(jax.random.key(seed), 2)
    kernel = draw_kernel(jax.random.fold_in(streams_of[1], 71), 0)
    return dict(kernel=kernel)


def reference(kernel):
    shape_in = kernel.shape
    order = shape_in[0] * shape_in[1] * shape_in[2]
    tile_size = shape_in[2]
    working = kernel.reshape(order, order)
    identity = jnp.eye(tile_size, dtype=jnp.float32)
    row_ids = jnp.arange(order)
    collected = []
    for panel_step in range(STEPS):
        start = panel_step * tile_size
        finish = start + tile_size
        factor = jnp.linalg.cholesky(working[start:finish, start:finish])
        inverse = lax.linalg.triangular_solve(factor, identity, left_side=True, lower=True)
        panel = jnp.dot(working[:, start:finish], inverse.T, precision=lax.Precision.HIGHEST)
        panel = jnp.where((row_ids >= start)[:, None], panel, jnp.float32(0.0))
        collected.append(panel)
        lower = panel[finish:]
        updated = working[finish:, finish:] - jnp.dot(lower, lower.T, precision=lax.Precision.HIGHEST)
        working = jnp.zeros((order, order), jnp.float32).at[finish:, finish:].set(updated)
    trailing = working.reshape(shape_in)
    panels = jnp.stack(collected, axis=1).reshape(shape_in[0], shape_in[1], tile_size, STEPS, tile_size)
    return (trailing, panels)
```

```python
import jax
import jax.numpy as jnp
from jax import lax
from jax.sharding import PartitionSpec as P

STEPS = 3
HIGHEST = lax.Precision.HIGHEST


def grid_perms(row_count, z_count, x_count):
    def col(move, keep=lambda z, x: True):
        pairs = []
        for z in range(z_count):
            for x in range(x_count):
                if keep(z, x):
                    z2, x2 = move(z, x)
                    pairs.append((z * x_count + x, (z2 % z_count) * x_count + x2 % x_count))
        return pairs

    def row(move):
        pairs = []
        for y in range(row_count // 2):
            for core in range(2):
                y2, core2 = move(y, core)
                pairs.append((y * 2 + core, (y2 % (row_count // 2)) * 2 + core2))
        return pairs

    return col, row


def unroll(parts, shift):
    count = len(parts)
    return lax.dynamic_slice_in_dim(jnp.stack(parts + parts), (count - shift) % count, count, 0)


def gather_row(piece, row, row_count):
    y_count = row_count // 2
    row_index = lax.axis_index("row")
    y = row_index // 2
    core = row_index % 2
    moved = [piece] + [
        lax.ppermute(piece, "row", row(lambda y, core, k=k: (y - k, core))) for k in range(1, y_count)
    ]
    mine = unroll(moved, y)
    other = lax.ppermute(mine, "row", row(lambda y, core: (y, 1 - core)))
    both = jnp.where(core == 0, jnp.stack([mine, other], 1), jnp.stack([other, mine], 1))
    return both.reshape((row_count,) + piece.shape)


def invert_factor(corner, tile):
    def dot(a, b):
        return jnp.dot(a, b, precision=HIGHEST)

    blocks = [[corner[i * tile:(i + 1) * tile, j * tile:(j + 1) * tile] for j in range(STEPS)] for i in range(STEPS)]
    identity = jnp.eye(tile, dtype=jnp.float32)
    inv = []
    low = [[None] * STEPS for _ in range(STEPS)]
    for k in range(STEPS):
        factor = jnp.linalg.cholesky(blocks[k][k])
        inv.append(lax.linalg.triangular_solve(factor, identity, left_side=True, lower=True))
        for i in range(k + 1, STEPS):
            low[i][k] = dot(blocks[i][k], inv[k].T)
        for i in range(k + 1, STEPS):
            for j in range(k + 1, i + 1):
                blocks[i][j] = blocks[i][j] - dot(low[i][k], low[j][k].T)
    zero = jnp.zeros((tile, tile), jnp.float32)
    i10 = -dot(inv[1], dot(low[1][0], inv[0]))
    i21 = -dot(inv[2], dot(low[2][1], inv[1]))
    i20 = -dot(inv[2], dot(low[2][0], inv[0]) + dot(low[2][1], i10))
    return jnp.block([[inv[0].T, i10.T, i20.T], [zero, inv[1].T, i21.T], [zero, zero, inv[2].T]])


def shards(kernel):
    row_tiles, _, tile, col_tiles, _, _ = kernel.shape
    row_count = lax.axis_size("row")
    col_count = lax.axis_size("col")
    row_index = lax.axis_index("row")
    col_index = lax.axis_index("col")
    x_count = 4
    z_count = col_count // x_count
    col, row = grid_perms(row_count, z_count, x_count)
    depth = STEPS * tile
    part = tile // row_count
    groups = col_count // row_count
    working = kernel.reshape(row_tiles, tile, col_tiles, tile)

    top = working[0].transpose(1, 2, 0).reshape(col_tiles, row_count, part, tile)
    top = top.transpose(1, 0, 2, 3)
    split = lax.all_to_all(top, "row", 0, 0, tiled=True)
    piece = split[:STEPS].transpose(1, 2, 0, 3).reshape(col_tiles, part, depth)

    cross = []
    for r in range(row_count):
        for c in range(col_count):
            g, c8 = divmod(c, row_count)
            cross.append((r * col_count + c, c8 * col_count + g * row_count + r))

    z = col_index // x_count
    x = col_index % x_count
    corner = jnp.where(z == 0, piece[0], 0.0)
    for level in (4, 2, 1):
        corner = corner + lax.ppermute(
            corner, "col",
            col(lambda z, x, s=level: (z + s, x), lambda z, x, s=level: z % (2 * s) == 0 and x < STEPS),
        )
    shifted = [corner] + [
        lax.ppermute(corner, "col", col(lambda z, x, k=k: (z, x - k))) for k in range(1, x_count)
    ]
    slices = unroll(shifted, x)[:STEPS]
    corner = gather_row(slices, row, row_count)
    corner = corner.transpose(1, 0, 2, 3).reshape(depth, depth)

    swapped = lax.ppermute(piece, ("row", "col"), cross)
    raw_cols = gather_row(piece, row, row_count)
    raw_cols = raw_cols.transpose(1, 0, 2, 3).reshape(col_tiles * tile, depth)
    raw_rows = lax.all_gather(swapped, "col", axis=0, tiled=False)
    raw_rows = raw_rows.reshape(groups, row_count, col_tiles, part, depth)
    raw_rows = raw_rows.transpose(2, 0, 1, 3, 4).reshape(row_tiles * tile, depth)

    upper = invert_factor(corner, tile)

    q = jnp.dot(raw_cols, upper, precision=HIGHEST)
    p = jnp.dot(raw_rows, upper, precision=HIGHEST)
    tile_rows = jnp.arange(row_tiles) * row_count + row_index
    tile_cols = jnp.arange(col_tiles) * col_count + col_index
    p = p.reshape(row_tiles, tile, STEPS, tile)
    correction = jnp.einsum(
        "atk,csk->atcs", p.reshape(row_tiles, tile, depth), q.reshape(col_tiles, tile, depth), precision=HIGHEST
    )
    keep = (tile_rows >= STEPS)[:, None, None, None] & (tile_cols >= STEPS)[None, None, :, None]
    trailing = jnp.where(keep, working - correction, 0.0).reshape(kernel.shape)
    panels = jnp.where(tile_rows[:, None, None, None] >= jnp.arange(STEPS)[None, None, :, None], p, 0.0)
    panels = panels.reshape(row_tiles, 1, tile, STEPS, tile)
    return (trailing, panels)


def solution(mesh):
    in_specs = (P(None, "row", None, None, "col", None),)
    out_specs = (P(None, "row", None, None, "col", None), P(None, "row", None, None, None))
    return jax.shard_map(shards, mesh=mesh, in_specs=in_specs, out_specs=out_specs, check_vma=False)
```

```python
import jax
import jax.numpy as jnp
from jax import lax
from jax.experimental import pallas as pl
from jax.experimental.pallas import tpu as pltpu
from jax.sharding import PartitionSpec as P

STEPS = 3
LANES = 128
SUBLANES = 8
HIGHEST = lax.Precision.HIGHEST


def grid_perms(row_count, z_count, x_count):
    def col(move, keep=lambda z, x: True):
        pairs = []
        for z in range(z_count):
            for x in range(x_count):
                if keep(z, x):
                    z2, x2 = move(z, x)
                    pairs.append((z * x_count + x, (z2 % z_count) * x_count + x2 % x_count))
        return pairs

    def row(move):
        pairs = []
        for y in range(row_count // 2):
            for core in range(2):
                y2, core2 = move(y, core)
                pairs.append((y * 2 + core, (y2 % (row_count // 2)) * 2 + core2))
        return pairs

    return col, row


def unroll(parts, shift):
    count = len(parts)
    return lax.dynamic_slice_in_dim(jnp.stack(parts + parts), (count - shift) % count, count, 0)


def gather_row(piece, row, row_count):
    y_count = row_count // 2
    row_index = lax.axis_index("row")
    y = row_index // 2
    core = row_index % 2
    moved = [piece] + [
        lax.ppermute(piece, "row", row(lambda y, core, k=k: (y - k, core))) for k in range(1, y_count)
    ]
    mine = unroll(moved, y)
    other = lax.ppermute(mine, "row", row(lambda y, core: (y, 1 - core)))
    both = jnp.where(core == 0, jnp.stack([mine, other], 1), jnp.stack([other, mine], 1))
    return both.reshape((row_count,) + piece.shape)


def product(a, b, dims):
    return lax.dot_general(a, b, (dims, ((), ())), precision=HIGHEST, preferred_element_type=jnp.float32)


def from_lane(v, lane):
    return jnp.broadcast_to(v[:, lane:lane + 1], (SUBLANES, LANES))


def from_row(v, row):
    return jnp.broadcast_to(v[row:row + 1, :], (SUBLANES, LANES))


def eliminate(t):
    count = len(t)
    rows = lax.broadcasted_iota(jnp.int32, (SUBLANES, LANES), 0)
    lanes = lax.broadcasted_iota(jnp.int32, (SUBLANES, LANES), 1)
    r = [jnp.where(lanes == rows + SUBLANES * k, jnp.float32(1.0), jnp.float32(0.0)) for k in range(count)]
    t = list(t)
    out = []
    for j in range(count):
        tj, rj = t[j], r[j]
        c = [from_lane(tj, SUBLANES * j + m) for m in range(SUBLANES)]
        e = {}
        inverse_pivots = []
        pivots = jnp.ones((SUBLANES, LANES), jnp.float32)
        for i in range(SUBLANES):
            d = from_row(c[i], i)
            pivots = jnp.where(rows == i, d, pivots)
            inverse_pivots.append(1.0 / d)
            f = jnp.where(rows > i, c[i] * inverse_pivots[i], 0.0)
            for m in range(i + 1, SUBLANES):
                e[i, m] = from_row(c[m], i)
                c[m] = c[m] - f * e[i, m]
            tj = tj - f * from_row(tj, i)
            rj = rj - f * from_row(rj, i)
        out.append(rj * lax.rsqrt(pivots))
        if j + 1 == count:
            break
        tb = [from_row(tj, i) for i in range(SUBLANES)]
        rb = [from_row(rj, i) for i in range(SUBLANES)]
        for k in range(j + 1, count):
            c = [from_lane(t[k], SUBLANES * j + m) for m in range(SUBLANES)]
            for i in range(SUBLANES):
                f = c[i] * inverse_pivots[i]
                for m in range(i + 1, SUBLANES):
                    c[m] = c[m] - f * e[i, m]
                t[k] = t[k] - f * tb[i]
                r[k] = r[k] - f * rb[i]
    return jnp.concatenate(out, 0)


def factor_kernel(corner_ref, inverse_ref):
    slices, _, part, depth = corner_ref.shape
    size = LANES
    blocks = depth // size
    per = size // part

    def corner(i, lo, hi):
        start = i * per
        return corner_ref[start % slices:start % slices + per, start // slices, :, lo:hi].reshape(size, hi - lo)

    cols = [
        jnp.concatenate([corner(i, s * size, (s + 1) * size) for i in range(s, blocks)], 0) for s in range(blocks)
    ]
    done = [None] * blocks
    for s in range(blocks):
        x = eliminate([cols[s][k:k + SUBLANES] for k in range(0, size, SUBLANES)])
        row = x if s == 0 else jnp.concatenate([product(x, -done[s], ((1,), (0,))), x], 1)
        inverse_ref[s * size:(s + 1) * size, :(s + 1) * size] = row
        if s + 1 == blocks:
            break
        inverse_ref[s * size:(s + 1) * size, (s + 1) * size:] = jnp.zeros((size, depth - (s + 1) * size), jnp.float32)
        low = product(cols[s][size:], x, ((1,), (1,)))
        for k in range(s + 1, blocks):
            at = (k - s - 1) * size
            cols[k] = cols[k] - product(low[at:], low[at:at + size], ((1,), (1,)))
        change = product(low, row, ((1,), (0,)))
        for k in range(s + 1, blocks):
            at = (k - s - 1) * size
            part_k = change[at:at + size]
            if s == 0:
                done[k] = part_k
            else:
                done[k] = jnp.concatenate([done[k] + part_k[:, :s * size], part_k[:, s * size:]], 1)


def invert_factor(corner):
    depth = corner.shape[-1]
    return pl.pallas_call(
        factor_kernel,
        out_shape=jax.ShapeDtypeStruct((depth, depth), jnp.float32),
        in_specs=[pl.BlockSpec(memory_space=pltpu.VMEM)],
        out_specs=pl.BlockSpec(memory_space=pltpu.VMEM),
        compiler_params=pltpu.CompilerParams(vmem_limit_bytes=40 << 20),
        cost_estimate=pl.CostEstimate(flops=8 * depth ** 3, bytes_accessed=8 * depth ** 2, transcendentals=0),
    )(corner)


def update_kernel(place_ref, old_ref, rows_ref, cols_ref, inverse_ref, new_ref, panels_ref, cols_panel):
    a = pl.program_id(0)
    tile = panels_ref.shape[2]
    depth = inverse_ref.shape[0]
    col_tiles = cols_ref.shape[1]

    def panel(raw, k):
        end = (k + 1) * tile
        return product(raw[:, :end], inverse_ref[k * tile:end, :end], ((1,), (1,)))

    @pl.when(a == 0)
    def _():
        for j in range(col_tiles):
            raw = cols_ref[:, j].reshape(tile, depth)
            for k in range(STEPS):
                cols_panel[j * tile:(j + 1) * tile, k * tile:(k + 1) * tile] = panel(raw, k)

    tile_row = a * place_ref[2] + place_ref[0]
    raw = rows_ref[0, :, 0].reshape(tile, depth)
    parts = [panel(raw, k) for k in range(STEPS)]
    for k in range(STEPS):
        panels_ref[0, k] = jnp.where(tile_row >= k, parts[k], 0.0)
    correction = product(jnp.concatenate(parts, 1), cols_panel[...], ((1,), (1,)))
    lane_blocks = tile // LANES
    for j in range(col_tiles):
        keep = jnp.logical_and(tile_row >= STEPS, j * place_ref[3] + place_ref[1] >= STEPS)
        for h in range(lane_blocks):
            at = pl.ds(j * lane_blocks + h, tile, stride=col_tiles * lane_blocks)
            lo = j * tile + h * LANES
            new_ref[0, at, :] = jnp.where(keep, old_ref[0, at, :] - correction[:, lo:lo + LANES], 0.0)


def update(place, old, rows, cols, inverse):
    row_tiles, lines, _ = old.shape
    groups, row_count, col_tiles, part, depth = rows.shape
    tile = row_count * part
    old_spec = pl.BlockSpec((1, lines, LANES), lambda a, s: (a, 0, 0))
    panels_spec = pl.BlockSpec((1, STEPS, tile, tile), lambda a, s: (a, 0, 0, 0))
    return pl.pallas_call(
        update_kernel,
        grid_spec=pltpu.PrefetchScalarGridSpec(
            num_scalar_prefetch=1,
            grid=(row_tiles,),
            in_specs=[
                old_spec,
                pl.BlockSpec((1, row_count, 1, part, depth), lambda a, s: (a % groups, 0, a // groups, 0, 0)),
                pl.BlockSpec((row_count, col_tiles, part, depth), lambda a, s: (0, 0, 0, 0)),
                pl.BlockSpec((depth, depth), lambda a, s: (0, 0)),
            ],
            out_specs=[old_spec, panels_spec],
            scratch_shapes=[pltpu.VMEM((col_tiles * tile, depth), jnp.float32)],
        ),
        out_shape=[
            jax.ShapeDtypeStruct(old.shape, jnp.float32),
            jax.ShapeDtypeStruct((row_tiles, STEPS, tile, tile), jnp.float32),
        ],
        compiler_params=pltpu.CompilerParams(vmem_limit_bytes=56 << 20),
        cost_estimate=pl.CostEstimate(
            flops=12 * row_tiles * tile * depth * depth, bytes_accessed=4 * (2 * old.size + 2 * rows.size), transcendentals=0
        ),
    )(place, old, rows, cols, inverse)


def shards(kernel):
    row_tiles, _, tile, col_tiles, _, _ = kernel.shape
    row_count = lax.axis_size("row")
    col_count = lax.axis_size("col")
    row_index = lax.axis_index("row")
    col_index = lax.axis_index("col")
    x_count = 4
    z_count = col_count // x_count
    col, row = grid_perms(row_count, z_count, x_count)
    depth = STEPS * tile
    part = tile // row_count
    groups = col_count // row_count

    top = kernel[0].reshape(tile, col_tiles, tile).transpose(1, 2, 0).reshape(col_tiles, row_count, part, tile)
    top = top.transpose(1, 0, 2, 3)
    split = lax.all_to_all(top, "row", 0, 0, tiled=True)
    piece = split[:STEPS].transpose(1, 2, 0, 3).reshape(col_tiles, part, depth)

    cross = []
    for r in range(row_count):
        for c in range(col_count):
            g, c8 = divmod(c, row_count)
            cross.append((r * col_count + c, c8 * col_count + g * row_count + r))

    z = col_index // x_count
    x = col_index % x_count
    corner = jnp.where(z == 0, piece[0], 0.0)
    for level in (4, 2, 1):
        corner = corner + lax.ppermute(
            corner, "col",
            col(lambda z, x, s=level: (z + s, x), lambda z, x, s=level: z % (2 * s) == 0 and x < STEPS),
        )
    shifted = [corner] + [
        lax.ppermute(corner, "col", col(lambda z, x, k=k: (z, x - k))) for k in range(1, x_count)
    ]
    slices = unroll(shifted, x)[:STEPS]
    corner = gather_row(slices, row, row_count)
    swapped = lax.ppermute(piece, ("row", "col"), cross)
    raw_cols = gather_row(piece, row, row_count)
    raw_rows = lax.all_gather(swapped, "col", axis=0, tiled=False)
    raw_rows = raw_rows.reshape(groups, row_count, col_tiles, part, depth)

    inverse = invert_factor(corner)

    place = jnp.stack([row_index, col_index, row_count, col_count]).astype(jnp.int32)
    old = kernel.reshape(row_tiles, tile * col_tiles * tile // LANES, LANES)
    trailing, panels = update(place, old, raw_rows, raw_cols, inverse)
    panels = panels.transpose(0, 2, 1, 3).reshape(row_tiles, 1, tile, STEPS, tile)
    return (trailing.reshape(kernel.shape), panels)


def solution(mesh):
    in_specs = (P(None, "row", None, None, "col", None),)
    out_specs = (P(None, "row", None, None, "col", None), P(None, "row", None, None, None))
    return jax.shard_map(shards, mesh=mesh, in_specs=in_specs, out_specs=out_specs, check_vma=False)
```

```python
import jax
import jax.numpy as jnp
from jax import lax
from jax.experimental import pallas as pl
from jax.experimental.pallas import tpu as pltpu
from jax.sharding import PartitionSpec as P

STEPS = 3
LANES = 128
SUBLANES = 8
HIGHEST = lax.Precision.HIGHEST


def grid_perms(row_count, z_count, x_count):
    def col(move, keep=lambda z, x: True):
        pairs = []
        for z in range(z_count):
            for x in range(x_count):
                if keep(z, x):
                    z2, x2 = move(z, x)
                    pairs.append((z * x_count + x, (z2 % z_count) * x_count + x2 % x_count))
        return pairs

    def row(move):
        pairs = []
        for y in range(row_count // 2):
            for core in range(2):
                y2, core2 = move(y, core)
                pairs.append((y * 2 + core, (y2 % (row_count // 2)) * 2 + core2))
        return pairs

    return col, row


def product(a, b, dims):
    return lax.dot_general(a, b, (dims, ((), ())), precision=HIGHEST, preferred_element_type=jnp.float32)


def from_lane(v, lane):
    return jnp.broadcast_to(v[:, lane:lane + 1], (SUBLANES, LANES))


def from_row(v, row):
    return jnp.broadcast_to(v[row:row + 1, :], (SUBLANES, LANES))


def eliminate(t):
    count = len(t)
    rows = lax.broadcasted_iota(jnp.int32, (SUBLANES, LANES), 0)
    lanes = lax.broadcasted_iota(jnp.int32, (SUBLANES, LANES), 1)
    r = [jnp.where(lanes == rows + SUBLANES * k, jnp.float32(1.0), jnp.float32(0.0)) for k in range(count)]
    t = list(t)
    out = []
    for j in range(count):
        tj, rj = t[j], r[j]
        c = [from_lane(tj, SUBLANES * j + m) for m in range(SUBLANES)]
        e = {}
        inverse_pivots = []
        pivots = jnp.ones((SUBLANES, LANES), jnp.float32)
        for i in range(SUBLANES):
            d = from_row(c[i], i)
            pivots = jnp.where(rows == i, d, pivots)
            inverse_pivots.append(1.0 / d)
            f = jnp.where(rows > i, c[i] * inverse_pivots[i], 0.0)
            for m in range(i + 1, SUBLANES):
                e[i, m] = from_row(c[m], i)
                c[m] = c[m] - f * e[i, m]
            tj = tj - f * from_row(tj, i)
            rj = rj - f * from_row(rj, i)
        out.append(rj * lax.rsqrt(pivots))
        if j + 1 == count:
            break
        tb = [from_row(tj, i) for i in range(SUBLANES)]
        rb = [from_row(rj, i) for i in range(SUBLANES)]
        for k in range(j + 1, count):
            c = [from_lane(t[k], SUBLANES * j + m) for m in range(SUBLANES)]
            for i in range(SUBLANES):
                f = c[i] * inverse_pivots[i]
                for m in range(i + 1, SUBLANES):
                    c[m] = c[m] - f * e[i, m]
                t[k] = t[k] - f * tb[i]
                r[k] = r[k] - f * rb[i]
    return jnp.concatenate(out, 0)


def place_rows(place_ref, mine_ref, other_ref, put):
    y_count = mine_ref.shape[0]
    y = place_ref[0] // 2
    core = place_ref[0] % 2
    for k in range(y_count):
        first = 2 * lax.rem(y + k, y_count)
        put(first + core, mine_ref[k])
        put(first + 1 - core, other_ref[k])


def factor_columns(column):
    size = LANES

    def inverse(block):
        return eliminate([block[k:k + SUBLANES] for k in range(0, size, SUBLANES)])

    left, right = column[:, :size], column[size:, size:]
    first = inverse(left[:size])
    low = product(left[size:], first, ((1,), (1,)))
    right = right - product(low, low[:size], ((1,), (1,)))
    second = inverse(right[:size])
    corner = -product(second, product(low[:size], first, ((1,), (0,))), ((1,), (0,)))
    inverse_factor = jnp.concatenate(
        [jnp.concatenate([first, jnp.zeros((size, size), jnp.float32)], 1), jnp.concatenate([corner, second], 1)], 0
    )
    if right.shape[0] == size:
        return inverse_factor, None
    return inverse_factor, jnp.concatenate([low[size:], product(right[size:], second, ((1,), (1,)))], 1)


def first_factor(place_ref, mine_ref, other_ref, inverse_ref, low_ref, column):
    tiles, part = mine_ref.shape[1:3]
    tile = column.shape[0] // tiles

    def put(slot, rows):
        for i in range(tiles):
            column[pl.ds(pl.multiple_of(i * tile + slot * part, part), part), :] = rows[i]

    place_rows(place_ref, mine_ref, other_ref, put)
    inverse_ref[...], low_ref[...] = factor_columns(column[...])


def second_factor(place_ref, mine_ref, other_ref, x0_ref, low0_ref, inverse_ref, low_ref, rest_ref, column):
    tiles, part = mine_ref.shape[1:3]
    tile = x0_ref.shape[0]

    def put(slot, rows):
        for i in range(tiles):
            column[pl.ds(pl.multiple_of(i * tile + slot * part, part), part), :] = rows[i]

    place_rows(place_ref, mine_ref, other_ref, put)
    low0 = low0_ref[...]
    inverse, low = factor_columns(column[:2 * tile] - product(low0, low0[:tile], ((1,), (1,))))
    rest_ref[...] = column[2 * tile:] - product(low0[tile:], low0[tile:], ((1,), (1,))) - product(low, low, ((1,), (1,)))
    low_ref[...] = low
    before = product(low0[:tile], x0_ref[...], ((1,), (0,)))
    inverse_ref[:, :tile] = -product(inverse, before, ((1,), (0,)))
    inverse_ref[:, tile:] = inverse


def third_factor(rest_ref, x0_ref, low0_ref, x1_ref, low1_ref, inverse_ref):
    tile = x0_ref.shape[0]
    inverse, _ = factor_columns(rest_ref[...])
    before = product(low1_ref[...], x1_ref[...], ((1,), (0,)))
    first = before[:, :tile] + product(low0_ref[tile:], x0_ref[...], ((1,), (0,)))
    inverse_ref[:, :tile] = -product(inverse, first, ((1,), (0,)))
    inverse_ref[:, tile:2 * tile] = -product(inverse, before[:, tile:], ((1,), (0,)))
    inverse_ref[:, 2 * tile:] = inverse


def local_call(kernel, out_shapes, args, scratch=(), scalars=True, micros=10):
    in_vmem = pl.BlockSpec(memory_space=pltpu.VMEM)
    specs = [in_vmem] * len(args)
    if scalars:
        specs[0] = pl.BlockSpec(memory_space=pltpu.SMEM)
    return pl.pallas_call(
        kernel,
        out_shape=[jax.ShapeDtypeStruct(shape, jnp.float32) for shape in out_shapes],
        in_specs=specs,
        out_specs=[in_vmem] * len(out_shapes),
        scratch_shapes=list(scratch),
        compiler_params=pltpu.CompilerParams(vmem_limit_bytes=24 << 20),
        cost_estimate=pl.CostEstimate(flops=micros * 1000 * 1000 * 1000, bytes_accessed=1 << 20, transcendentals=0),
    )(*args)


def update_kernel(first, shifts, place_ref, old_ref, *refs):
    step = pl.program_id(0)
    rows_refs, refs = refs[:len(shifts)], refs[len(shifts):]
    inverses, refs = refs[:STEPS], refs[STEPS:]
    z_count, _, col_tiles, part, tile = rows_refs[0].shape
    span = z_count // 2
    if first:
        mine_ref, other_ref, new_ref, panels_ref, cols_panel, cols = refs

        @pl.when(step == 0)
        def _():
            def put(slot, rows):
                for k in range(STEPS):
                    for j in range(col_tiles):
                        at = pl.ds(pl.multiple_of(j * tile + slot * part, part), part)
                        cols[at, k * tile:(k + 1) * tile] = rows[k, j]

            place_rows(place_ref, mine_ref, other_ref, put)
            for k in range(STEPS):
                end = (k + 1) * tile
                cols_panel[:, k * tile:end] = product(cols[:, :end], inverses[k][...], ((1,), (1,)))
    else:
        cols_panel, _, _, new_ref, panels_ref = refs

    z_first = span * (step % 2)
    x_count = place_ref[2] // z_count
    z_here = place_ref[1] // x_count
    spots = [lax.rem(z_first + i - z_here + z_count, z_count) for i in range(span)]

    def slices(k, j, i):
        value = rows_refs[0][spots[i], k, j]
        for n in range(1, len(shifts)):
            value = jnp.where(step // 2 == n, rows_refs[n][spots[i], k, j], value)
        return value

    raw = jnp.concatenate(
        [
            jnp.concatenate([slices(k, j, i) for j in range(col_tiles) for i in range(span)], 0)
            for k in range(STEPS)
        ],
        1,
    )
    parts = [product(raw[:, :(k + 1) * tile], inverses[k][...], ((1,), (1,))) for k in range(STEPS)]
    correction = product(jnp.concatenate(parts, 1), cols_panel[...], ((1,), (1,)))
    lane_blocks = tile // LANES
    groups = z_count // 2
    for n in range(col_tiles):
        for i in range(span):
            g, half = divmod(i, 2)
            top = (n * span + i) * part
            tile_row = (n * groups + z_first // 2 + g) * place_ref[3] + place_ref[0]
            for k in range(STEPS):
                panels_ref[n, g, k, half, 0] = jnp.where(tile_row >= k, parts[k][top:top + part], 0.0)
            for j in range(col_tiles):
                keep = jnp.logical_and(tile_row >= STEPS, j * place_ref[2] + place_ref[1] >= STEPS)
                for h in range(lane_blocks):
                    at = pl.ds(j * lane_blocks + h, part, stride=col_tiles * lane_blocks)
                    lo = j * tile + h * LANES
                    fresh = old_ref[n, g, half, 0, at, :] - correction[top:top + part, lo:lo + LANES]
                    new_ref[n, g, half, 0, at, :] = jnp.where(keep, fresh, 0.0)


def update(place, old, rows, shifts, inverses, extra):
    halves, groups, _, x_count, lines, _ = old.shape
    z_count, _, col_tiles, part, tile = rows[0].shape
    depth = STEPS * tile
    first = shifts[0] == 0
    steps = 2 * len(shifts)

    def spot(step, s):
        shift = shifts[0]
        for n in range(1, len(shifts)):
            shift = jnp.where(step // 2 == n, shifts[n], shift)
        return lax.rem(s[1] + shift, x_count)

    whole = pl.BlockSpec(memory_space=pltpu.VMEM)
    old_spec = pl.BlockSpec(
        (halves, groups // 2, 2, 1, lines, LANES), lambda d, s: (0, d % 2, 0, spot(d, s), 0, 0)
    )
    panels_shape = (halves, groups, STEPS, 2, x_count, part, tile)
    panels_spec = pl.BlockSpec(
        (halves, groups // 2, STEPS, 2, 1, part, tile), lambda d, s: (0, d % 2, 0, 0, spot(d, s), 0, 0)
    )
    scratch = []
    out_specs = [old_spec, panels_spec]
    out_shape = [jax.ShapeDtypeStruct(old.shape, jnp.float32), jax.ShapeDtypeStruct(panels_shape, jnp.float32)]
    extra_specs = [whole] * len(extra)
    aliases = {}
    if first:
        scratch = [pltpu.VMEM((col_tiles * tile, depth), jnp.float32)]
        out_specs.append(pl.BlockSpec((col_tiles * tile, depth), lambda d, s: (0, 0)))
        out_shape.append(jax.ShapeDtypeStruct((col_tiles * tile, depth), jnp.float32))
    else:
        extra_specs[1:] = [pl.BlockSpec(memory_space=pl.ANY)] * 2
        at = 2 + len(rows) + STEPS + 1
        aliases = {at: 0, at + 1: 1}
    return pl.pallas_call(
        lambda *refs: update_kernel(first, shifts, *refs),
        grid_spec=pltpu.PrefetchScalarGridSpec(
            num_scalar_prefetch=1,
            grid=(steps,),
            in_specs=[old_spec] + [whole] * (len(rows) + STEPS) + extra_specs,
            out_specs=out_specs,
            scratch_shapes=scratch,
        ),
        out_shape=out_shape,
        input_output_aliases=aliases,
        compiler_params=pltpu.CompilerParams(vmem_limit_bytes=40 << 20),
        cost_estimate=pl.CostEstimate(
            flops=4 * steps * 1000 * 1000 * 1000, bytes_accessed=steps << 20, transcendentals=0
        ),
    )(place, old, *rows, *inverses, *extra)


def in_order(index, parts, wanted):
    count = len(parts)

    def pick(place):
        value = parts[place % count]
        for at in range(1, count):
            value = jnp.where(index == at, parts[(place - at) % count], value)
        return value

    return jnp.stack([pick(place) for place in wanted])


def shards(kernel):
    row_tiles, _, tile, col_tiles, _, _ = kernel.shape
    row_count = lax.axis_size("row")
    col_count = lax.axis_size("col")
    row_index = lax.axis_index("row")
    col_index = lax.axis_index("col")
    x_count = 4
    y_count = row_count // 2
    z_count = col_count // x_count
    col, row = grid_perms(row_count, z_count, x_count)
    depth = STEPS * tile
    part = tile // row_count
    groups = col_count // row_count
    place = jnp.stack([row_index, col_index, jnp.int32(col_count), jnp.int32(row_count)]).astype(jnp.int32)

    def from_z(value, k):
        return lax.ppermute(value, "col", col(lambda z, x: (z - k, x)))

    def from_x(value, k):
        return lax.ppermute(value, "col", col(lambda z, x: (z, x - k)))

    def from_y(value, k):
        return lax.ppermute(value, "row", row(lambda y, core: (y - k, core)))

    def over_rows(value):
        mine = jnp.stack([value] + [from_y(value, k) for k in range(1, y_count)])
        return mine, lax.ppermute(mine, "row", row(lambda y, core: (y, 1 - core)))

    top = kernel[0].reshape(tile, col_tiles, row_count, part).transpose(2, 1, 3, 0)
    piece = lax.all_to_all(top, "row", 0, 0, tiled=True)[:STEPS]

    cross = []
    for r in range(row_count):
        for c in range(col_count):
            g, c8 = divmod(c, row_count)
            cross.append((r * col_count + c, c8 * col_count + g * row_count + r))

    z = col_index // x_count
    x = col_index % x_count
    swapped = lax.ppermute(piece, ("row", "col"), cross)
    corner = jnp.where(z == 0, piece[:, 0], 0.0)
    level = z_count // 2
    while level:
        corner = corner + lax.ppermute(
            corner, "col", col(lambda z, x: (z + level, x), lambda z, x: z % (2 * level) == 0 and x < STEPS)
        )
        level //= 2
    corner, swapped = lax.optimization_barrier((corner, swapped))
    corner = in_order(x, [corner] + [from_x(corner, k) for k in range(1, x_count)], range(STEPS))
    early = over_rows(corner[:, 0])
    late = jnp.stack([corner[1, 1], corner[2, 1], corner[2, 2]])
    late, _ = lax.optimization_barrier((late, early[0]))
    late = over_rows(late)

    ups, downs = [swapped], [swapped]
    for k in range(1, z_count // 2):
        ups.append(from_z(ups[-1], -1))
        downs.append(from_z(downs[-1], 1))
    far = jnp.concatenate([from_z(ups[-1][:, :1], -1), from_z(downs[-1][:, 1:], 1)], 1)
    here = jnp.stack(downs + [far] + ups[:0:-1])
    right, left = from_x(here, 1), from_x(here, -1)
    across = jnp.concatenate([from_x(right[:z_count // 2], 1), from_x(left[z_count // 2:], -1)])

    column = pltpu.VMEM((depth, tile), jnp.float32)
    x0, low0 = local_call(first_factor, [(tile, tile), (depth - tile, tile)], (place,) + early, [column])
    piece, _ = lax.optimization_barrier((piece, x0))
    cols = over_rows(piece)
    x1, low1, rest = local_call(
        second_factor, [(tile, 2 * tile), (tile, tile), (tile, tile)], (place,) + late + (x0, low0), [column]
    )
    x2, = local_call(third_factor, [(tile, depth)], (rest, x0, low0, x1, low1), scalars=False)

    old = kernel.reshape(col_tiles, groups, 2, x_count, part * col_tiles * tile // LANES, LANES)
    inverses = (x0, x1, x2)
    trailing, panels, cols_panel = update(place, old, [here], (0,), inverses, cols)
    trailing, panels = update(place, old, [right, left], (1, x_count - 1), inverses, (cols_panel, trailing, panels))
    trailing, panels = update(place, old, [across], (2,), inverses, (cols_panel, trailing, panels))
    panels = panels.reshape(row_tiles, STEPS, tile, tile).transpose(0, 2, 1, 3).reshape(row_tiles, 1, tile, STEPS, tile)
    return (trailing.reshape(kernel.shape), panels)


def solution(mesh):
    in_specs = (P(None, "row", None, None, "col", None),)
    out_specs = (P(None, "row", None, None, "col", None), P(None, "row", None, None, None))
    return jax.shard_map(shards, mesh=mesh, in_specs=in_specs, out_specs=out_specs, check_vma=False)
```

```python
import jax
import jax.numpy as jnp
from jax import lax
from jax.experimental import pallas as pl
from jax.experimental.pallas import tpu as pltpu
from jax.sharding import PartitionSpec as P

STEPS = 3
LANES = 128
SUBLANES = 8
HIGHEST = lax.Precision.HIGHEST


def grid_perms(row_count, z_count, x_count):
    def col(move, keep=lambda z, x: True):
        pairs = []
        for z in range(z_count):
            for x in range(x_count):
                if keep(z, x):
                    z2, x2 = move(z, x)
                    pairs.append((z * x_count + x, (z2 % z_count) * x_count + x2 % x_count))
        return pairs

    def row(move):
        pairs = []
        for y in range(row_count // 2):
            for core in range(2):
                y2, core2 = move(y, core)
                pairs.append((y * 2 + core, (y2 % (row_count // 2)) * 2 + core2))
        return pairs

    return col, row


def product(a, b, dims):
    return lax.dot_general(a, b, (dims, ((), ())), precision=HIGHEST, preferred_element_type=jnp.float32)


def from_lane(v, lane):
    return jnp.broadcast_to(v[:, lane:lane + 1], (SUBLANES, LANES))


def from_row(v, row):
    return jnp.broadcast_to(v[row:row + 1, :], (SUBLANES, LANES))


def eliminate(t):
    count = len(t)
    rows = lax.broadcasted_iota(jnp.int32, (SUBLANES, LANES), 0)
    lanes = lax.broadcasted_iota(jnp.int32, (SUBLANES, LANES), 1)
    r = [jnp.where(lanes == rows + SUBLANES * k, jnp.float32(1.0), jnp.float32(0.0)) for k in range(count)]
    t = list(t)
    out = []
    for j in range(count):
        tj, rj = t[j], r[j]
        c = [from_lane(tj, SUBLANES * j + m) for m in range(SUBLANES)]
        e = {}
        inverse_pivots = []
        pivots = jnp.ones((SUBLANES, LANES), jnp.float32)
        for i in range(SUBLANES):
            d = from_row(c[i], i)
            pivots = jnp.where(rows == i, d, pivots)
            inverse_pivots.append(1.0 / d)
            f = jnp.where(rows > i, c[i] * inverse_pivots[i], 0.0)
            for m in range(i + 1, SUBLANES):
                e[i, m] = from_row(c[m], i)
                c[m] = c[m] - f * e[i, m]
            tj = tj - f * from_row(tj, i)
            rj = rj - f * from_row(rj, i)
        out.append(rj * lax.rsqrt(pivots))
        if j + 1 == count:
            break
        tb = [from_row(tj, i) for i in range(SUBLANES)]
        rb = [from_row(rj, i) for i in range(SUBLANES)]
        for k in range(j + 1, count):
            c = [from_lane(t[k], SUBLANES * j + m) for m in range(SUBLANES)]
            for i in range(SUBLANES):
                f = c[i] * inverse_pivots[i]
                for m in range(i + 1, SUBLANES):
                    c[m] = c[m] - f * e[i, m]
                t[k] = t[k] - f * tb[i]
                r[k] = r[k] - f * rb[i]
    return jnp.concatenate(out, 0)


def place_rows(place_ref, mine_ref, other_ref, put):
    y_count = mine_ref.shape[0]
    y = place_ref[0] // 2
    core = place_ref[0] % 2
    for k in range(y_count):
        first = 2 * lax.rem(y + k, y_count)
        put(first + core, mine_ref[k])
        put(first + 1 - core, other_ref[k])


def factor_columns(column):
    size = LANES

    def inverse(block):
        return eliminate([block[k:k + SUBLANES] for k in range(0, size, SUBLANES)])

    left, right = column[:, :size], column[size:, size:]
    first = inverse(left[:size])
    low = product(left[size:], first, ((1,), (1,)))
    right = right - product(low, low[:size], ((1,), (1,)))
    second = inverse(right[:size])
    corner = -product(second, product(low[:size], first, ((1,), (0,))), ((1,), (0,)))
    inverse_factor = jnp.concatenate(
        [jnp.concatenate([first, jnp.zeros((size, size), jnp.float32)], 1), jnp.concatenate([corner, second], 1)], 0
    )
    if right.shape[0] == size:
        return inverse_factor, None
    return inverse_factor, jnp.concatenate([low[size:], product(right[size:], second, ((1,), (1,)))], 1)


def factor_kernel(place_ref, mine_ref, other_ref, x0_ref, x1_ref, x2_ref, corner):
    tiles, part = mine_ref.shape[1:3]
    tile = x0_ref.shape[0]

    def put(slot, rows):
        for i in range(tiles):
            corner[pl.ds(pl.multiple_of(i * tile + slot * part, part), part), :] = rows[i]

    place_rows(place_ref, mine_ref, other_ref, put)
    x0, low0 = factor_columns(corner[:3 * tile])
    x0_ref[...] = x0
    x1, low1 = factor_columns(corner[3 * tile:5 * tile] - product(low0, low0[:tile], ((1,), (1,))))
    rest = corner[5 * tile:] - product(low0[tile:], low0[tile:], ((1,), (1,)))
    x2, _ = factor_columns(rest - product(low1, low1, ((1,), (1,))))
    before = product(low0, x0, ((1,), (0,)))
    row1 = jnp.concatenate([-product(x1, before[:tile], ((1,), (0,))), x1], 1)
    x1_ref[...] = row1
    past = product(low1, row1, ((1,), (0,)))
    x2_ref[:, :tile] = -product(x2, before[tile:] + past[:, :tile], ((1,), (0,)))
    x2_ref[:, tile:2 * tile] = -product(x2, past[:, tile:], ((1,), (0,)))
    x2_ref[:, 2 * tile:] = x2


def local_call(kernel, out_shapes, args, scratch=(), micros=30):
    in_vmem = pl.BlockSpec(memory_space=pltpu.VMEM)
    specs = [pl.BlockSpec(memory_space=pltpu.SMEM)] + [in_vmem] * (len(args) - 1)
    return pl.pallas_call(
        kernel,
        out_shape=[jax.ShapeDtypeStruct(shape, jnp.float32) for shape in out_shapes],
        in_specs=specs,
        out_specs=[in_vmem] * len(out_shapes),
        scratch_shapes=list(scratch),
        compiler_params=pltpu.CompilerParams(vmem_limit_bytes=32 << 20),
        cost_estimate=pl.CostEstimate(flops=micros * 1000 * 1000 * 1000, bytes_accessed=1 << 20, transcendentals=0),
    )(*args)


def update_kernel(first, shifts, place_ref, old_ref, *refs):
    step = pl.program_id(0)
    rows_refs, refs = refs[:len(shifts)], refs[len(shifts):]
    inverses, refs = refs[:STEPS], refs[STEPS:]
    z_count, _, col_tiles, part, tile = rows_refs[0].shape
    span = z_count // 2
    if first:
        mine_ref, other_ref, new_ref, panels_ref, cols_panel, cols = refs

        @pl.when(step == 0)
        def _():
            def put(slot, rows):
                for k in range(STEPS):
                    for j in range(col_tiles):
                        at = pl.ds(pl.multiple_of(j * tile + slot * part, part), part)
                        cols[at, k * tile:(k + 1) * tile] = rows[k, j]

            place_rows(place_ref, mine_ref, other_ref, put)
            for k in range(STEPS):
                end = (k + 1) * tile
                cols_panel[:, k * tile:end] = product(cols[:, :end], inverses[k][...], ((1,), (1,)))
    else:
        cols_panel, _, _, new_ref, panels_ref = refs

    z_first = span * (step % 2)
    x_count = place_ref[2] // z_count
    z_here = place_ref[1] // x_count
    spots = [lax.rem(z_first + i - z_here + z_count, z_count) for i in range(span)]

    def slices(k, j, i):
        value = rows_refs[0][spots[i], k, j]
        for n in range(1, len(shifts)):
            value = jnp.where(step // 2 == n, rows_refs[n][spots[i], k, j], value)
        return value

    raw = jnp.concatenate(
        [
            jnp.concatenate([slices(k, j, i) for j in range(col_tiles) for i in range(span)], 0)
            for k in range(STEPS)
        ],
        1,
    )
    parts = [product(raw[:, :(k + 1) * tile], inverses[k][...], ((1,), (1,))) for k in range(STEPS)]
    correction = product(jnp.concatenate(parts, 1), cols_panel[...], ((1,), (1,)))
    lane_blocks = tile // LANES
    groups = z_count // 2
    for n in range(col_tiles):
        for i in range(span):
            g, half = divmod(i, 2)
            top = (n * span + i) * part
            tile_row = (n * groups + z_first // 2 + g) * place_ref[3] + place_ref[0]
            for k in range(STEPS):
                panels_ref[n, g, k, half, 0] = jnp.where(tile_row >= k, parts[k][top:top + part], 0.0)
            for j in range(col_tiles):
                keep = jnp.logical_and(tile_row >= STEPS, j * place_ref[2] + place_ref[1] >= STEPS)
                for h in range(lane_blocks):
                    at = pl.ds(j * lane_blocks + h, part, stride=col_tiles * lane_blocks)
                    lo = j * tile + h * LANES
                    fresh = old_ref[n, g, half, 0, at, :] - correction[top:top + part, lo:lo + LANES]
                    new_ref[n, g, half, 0, at, :] = jnp.where(keep, fresh, 0.0)


def update(place, old, rows, shifts, inverses, extra):
    halves, groups, _, x_count, lines, _ = old.shape
    z_count, _, col_tiles, part, tile = rows[0].shape
    depth = STEPS * tile
    first = shifts[0] == 0
    steps = 2 * len(shifts)

    def spot(step, s):
        shift = shifts[0]
        for n in range(1, len(shifts)):
            shift = jnp.where(step // 2 == n, shifts[n], shift)
        return lax.rem(s[1] + shift, x_count)

    whole = pl.BlockSpec(memory_space=pltpu.VMEM)
    old_spec = pl.BlockSpec(
        (halves, groups // 2, 2, 1, lines, LANES), lambda d, s: (0, d % 2, 0, spot(d, s), 0, 0)
    )
    panels_shape = (halves, groups, STEPS, 2, x_count, part, tile)
    panels_spec = pl.BlockSpec(
        (halves, groups // 2, STEPS, 2, 1, part, tile), lambda d, s: (0, d % 2, 0, 0, spot(d, s), 0, 0)
    )
    scratch = []
    out_specs = [old_spec, panels_spec]
    out_shape = [jax.ShapeDtypeStruct(old.shape, jnp.float32), jax.ShapeDtypeStruct(panels_shape, jnp.float32)]
    extra_specs = [whole] * len(extra)
    aliases = {}
    if first:
        scratch = [pltpu.VMEM((col_tiles * tile, depth), jnp.float32)]
        out_specs.append(pl.BlockSpec((col_tiles * tile, depth), lambda d, s: (0, 0)))
        out_shape.append(jax.ShapeDtypeStruct((col_tiles * tile, depth), jnp.float32))
    else:
        extra_specs[1:] = [pl.BlockSpec(memory_space=pl.ANY)] * 2
        at = 2 + len(rows) + STEPS + 1
        aliases = {at: 0, at + 1: 1}
    return pl.pallas_call(
        lambda *refs: update_kernel(first, shifts, *refs),
        grid_spec=pltpu.PrefetchScalarGridSpec(
            num_scalar_prefetch=1,
            grid=(steps,),
            in_specs=[old_spec] + [whole] * (len(rows) + STEPS) + extra_specs,
            out_specs=out_specs,
            scratch_shapes=scratch,
        ),
        out_shape=out_shape,
        input_output_aliases=aliases,
        compiler_params=pltpu.CompilerParams(vmem_limit_bytes=40 << 20),
        cost_estimate=pl.CostEstimate(
            flops=4 * steps * 1000 * 1000 * 1000, bytes_accessed=steps << 20, transcendentals=0
        ),
    )(place, old, *rows, *inverses, *extra)


def in_order(index, parts, wanted):
    count = len(parts)

    def pick(place):
        value = parts[place % count]
        for at in range(1, count):
            value = jnp.where(index == at, parts[(place - at) % count], value)
        return value

    return [pick(place) for place in wanted]


def shards(kernel):
    row_tiles, _, tile, col_tiles, _, _ = kernel.shape
    row_count = lax.axis_size("row")
    col_count = lax.axis_size("col")
    row_index = lax.axis_index("row")
    col_index = lax.axis_index("col")
    x_count = 4
    y_count = row_count // 2
    z_count = col_count // x_count
    col, row = grid_perms(row_count, z_count, x_count)
    depth = STEPS * tile
    part = tile // row_count
    groups = col_count // row_count
    place = jnp.stack([row_index, col_index, jnp.int32(col_count), jnp.int32(row_count)]).astype(jnp.int32)

    def from_z(value, k):
        return lax.ppermute(value, "col", col(lambda z, x: (z - k, x)))

    def from_x(value, k):
        return lax.ppermute(value, "col", col(lambda z, x: (z, x - k)))

    def from_y(value, k):
        return lax.ppermute(value, "row", row(lambda y, core: (y - k, core)))

    top = kernel[0].reshape(tile, col_tiles, row_count, part).transpose(2, 1, 3, 0)
    piece = lax.all_to_all(top, "row", 0, 0, tiled=True)[:STEPS]

    cross = []
    for r in range(row_count):
        for c in range(col_count):
            g, c8 = divmod(c, row_count)
            cross.append((r * col_count + c, c8 * col_count + g * row_count + r))

    z = col_index // x_count
    x = col_index % x_count

    def from_rows(value):
        return [value] + [from_y(value, k) for k in range(1, y_count)]

    def from_core(value):
        return lax.ppermute(value, "row", row(lambda y, core: (y, 1 - core)))

    def spread(value, level):
        moved = lax.ppermute(
            value, "col", col(lambda z, x: (z + level, x), lambda z, x: z % (2 * level) == 0 and x < STEPS)
        )
        return value + moved

    stage = lax.optimization_barrier
    swapped = lax.ppermute(piece, ("row", "col"), cross)
    corner = jnp.where(z == 0, piece[:, 0], 0.0)
    level = z_count // 2
    while level > 1:
        corner = spread(corner, level)
        level //= 2
    corner, swapped, piece = stage((corner, swapped, piece))

    ups, downs = [swapped], [swapped]

    def relay():
        ups.append(from_z(ups[-1], -1))
        downs.append(from_z(downs[-1], 1))

    corner = spread(corner, level)
    relay()
    cols = from_rows(piece)
    corner, ups[-1], downs[-1] = stage((corner, ups[-1], downs[-1]))

    corner = [corner] + [from_x(corner, k) for k in range(1, x_count)]
    relay()
    corner, ups[-1], downs[-1], cols = stage((corner, ups[-1], downs[-1], cols))
    cols = jnp.stack(cols)
    cols = [cols, from_core(cols)]

    corner = in_order(x, corner, range(STEPS))
    tiles = from_rows(jnp.stack([corner[i][k] for k in range(STEPS) for i in range(k, STEPS)]))
    relay()
    tiles, ups[-1], downs[-1] = stage((tiles, ups[-1], downs[-1]))

    mine = jnp.stack(tiles)
    other = from_core(mine)
    far = jnp.concatenate([from_z(ups[-1][:, :1], -1), from_z(downs[-1][:, 1:], 1)], 1)
    here = jnp.stack(downs + [far] + ups[:0:-1])
    other, here, cols = stage((other, here, cols))

    right, left = from_x(here, 1), from_x(here, -1)
    x0, x1, x2 = local_call(
        factor_kernel,
        [(tile, (k + 1) * tile) for k in range(STEPS)],
        (place, mine, other),
        [pltpu.VMEM((tiles[0].shape[0] * tile, tile), jnp.float32)],
    )

    x0, right, left = stage((x0, right, left))
    across = jnp.concatenate([from_x(right[:z_count // 2], 1), from_x(left[z_count // 2:], -1)])
    old = kernel.reshape(col_tiles, groups, 2, x_count, part * col_tiles * tile // LANES, LANES)
    inverses = (x0, x1, x2)
    trailing, panels, cols_panel = update(place, old, [here], (0,), inverses, cols)
    trailing, panels = update(place, old, [right, left], (1, x_count - 1), inverses, (cols_panel, trailing, panels))
    trailing, panels = update(place, old, [across], (2,), inverses, (cols_panel, trailing, panels))
    panels = panels.reshape(row_tiles, STEPS, tile, tile).transpose(0, 2, 1, 3).reshape(row_tiles, 1, tile, STEPS, tile)
    return (trailing.reshape(kernel.shape), panels)


def solution(mesh):
    in_specs = (P(None, "row", None, None, "col", None),)
    out_specs = (P(None, "row", None, None, "col", None), P(None, "row", None, None, None))
    return jax.shard_map(shards, mesh=mesh, in_specs=in_specs, out_specs=out_specs, check_vma=False)
```

```python
import jax
import jax.numpy as jnp
from jax import lax
from jax.experimental import pallas as pl
from jax.experimental.pallas import tpu as pltpu
from jax.sharding import PartitionSpec as P

STEPS = 3
LANES = 128
SUBLANES = 8
HIGHEST = lax.Precision.HIGHEST


def grid_perms(row_count, z_count, x_count):
    def col(move, keep=lambda z, x: True):
        pairs = []
        for z in range(z_count):
            for x in range(x_count):
                if keep(z, x):
                    z2, x2 = move(z, x)
                    pairs.append((z * x_count + x, (z2 % z_count) * x_count + x2 % x_count))
        return pairs

    def row(move):
        pairs = []
        for y in range(row_count // 2):
            for core in range(2):
                y2, core2 = move(y, core)
                pairs.append((y * 2 + core, (y2 % (row_count // 2)) * 2 + core2))
        return pairs

    return col, row


def product(a, b, dims):
    return lax.dot_general(a, b, (dims, ((), ())), precision=HIGHEST, preferred_element_type=jnp.float32)


def from_lane(v, lane):
    return jnp.broadcast_to(v[:, lane:lane + 1], (SUBLANES, LANES))


def from_row(v, row):
    return jnp.broadcast_to(v[row:row + 1, :], (SUBLANES, LANES))


def eliminate(t):
    count = len(t)
    rows = lax.broadcasted_iota(jnp.int32, (SUBLANES, LANES), 0)
    lanes = lax.broadcasted_iota(jnp.int32, (SUBLANES, LANES), 1)
    r = [jnp.where(lanes == rows + SUBLANES * k, jnp.float32(1.0), jnp.float32(0.0)) for k in range(count)]
    t = list(t)
    out = []
    for j in range(count):
        tj, rj = t[j], r[j]
        c = [from_lane(tj, SUBLANES * j + m) for m in range(SUBLANES)]
        e = {}
        inverse_pivots = []
        pivots = jnp.ones((SUBLANES, LANES), jnp.float32)
        for i in range(SUBLANES):
            d = from_row(c[i], i)
            pivots = jnp.where(rows == i, d, pivots)
            inverse_pivots.append(1.0 / d)
            f = jnp.where(rows > i, c[i] * inverse_pivots[i], 0.0)
            for m in range(i + 1, SUBLANES):
                e[i, m] = from_row(c[m], i)
                c[m] = c[m] - f * e[i, m]
            tj = tj - f * from_row(tj, i)
            rj = rj - f * from_row(rj, i)
        out.append(rj * lax.rsqrt(pivots))
        if j + 1 == count:
            break
        tb = [from_row(tj, i) for i in range(SUBLANES)]
        rb = [from_row(rj, i) for i in range(SUBLANES)]
        for k in range(j + 1, count):
            c = [from_lane(t[k], SUBLANES * j + m) for m in range(SUBLANES)]
            for i in range(SUBLANES):
                f = c[i] * inverse_pivots[i]
                for m in range(i + 1, SUBLANES):
                    c[m] = c[m] - f * e[i, m]
                t[k] = t[k] - f * tb[i]
                r[k] = r[k] - f * rb[i]
    return jnp.concatenate(out, 0)


def place_rows(place_ref, mine_ref, other_ref, put):
    y_count = mine_ref.shape[0]
    y = place_ref[0] // 2
    core = place_ref[0] % 2
    for k in range(y_count):
        first = 2 * lax.rem(y + k, y_count)
        put(first + core, mine_ref[k])
        put(first + 1 - core, other_ref[k])


def factor_columns(column):
    size = LANES

    def inverse(block):
        return eliminate([block[k:k + SUBLANES] for k in range(0, size, SUBLANES)])

    left, right = column[:, :size], column[size:, size:]
    first = inverse(left[:size])
    low = product(left[size:], first, ((1,), (1,)))
    right = right - product(low, low[:size], ((1,), (1,)))
    second = inverse(right[:size])
    corner = -product(second, product(low[:size], first, ((1,), (0,))), ((1,), (0,)))
    inverse_factor = jnp.concatenate(
        [jnp.concatenate([first, jnp.zeros((size, size), jnp.float32)], 1), jnp.concatenate([corner, second], 1)], 0
    )
    if right.shape[0] == size:
        return inverse_factor, None
    return inverse_factor, jnp.concatenate([low[size:], product(right[size:], second, ((1,), (1,)))], 1)


def first_factor(place_ref, mine_ref, other_ref, inverse_ref, low_ref, rest_ref, corner):
    tiles, part = mine_ref.shape[1:3]
    tile = inverse_ref.shape[0]

    def put(slot, rows):
        for i in range(tiles):
            corner[pl.ds(pl.multiple_of(i * tile + slot * part, part), part), :] = rows[i]

    place_rows(place_ref, mine_ref, other_ref, put)
    inverse_ref[...], low = factor_columns(corner[:3 * tile])
    low_ref[...] = low
    rest_ref[:2 * tile] = corner[3 * tile:5 * tile] - product(low, low[:tile], ((1,), (1,)))
    rest_ref[2 * tile:] = corner[5 * tile:] - product(low[tile:], low[tile:], ((1,), (1,)))


def second_factor(rest_ref, x0_ref, low0_ref, inverse_ref, low_ref, last_ref):
    tile = x0_ref.shape[0]
    inverse, low = factor_columns(rest_ref[:2 * tile])
    low_ref[...] = low
    last_ref[...] = rest_ref[2 * tile:] - product(low, low, ((1,), (1,)))
    before = product(low0_ref[:tile], x0_ref[...], ((1,), (0,)))
    inverse_ref[:, :tile] = -product(inverse, before, ((1,), (0,)))
    inverse_ref[:, tile:] = inverse


def third_factor(last_ref, x0_ref, low0_ref, x1_ref, low1_ref, inverse_ref):
    tile = x0_ref.shape[0]
    inverse, _ = factor_columns(last_ref[...])
    before = product(low1_ref[...], x1_ref[...], ((1,), (0,)))
    first = before[:, :tile] + product(low0_ref[tile:], x0_ref[...], ((1,), (0,)))
    inverse_ref[:, :tile] = -product(inverse, first, ((1,), (0,)))
    inverse_ref[:, tile:2 * tile] = -product(inverse, before[:, tile:], ((1,), (0,)))
    inverse_ref[:, 2 * tile:] = inverse


def local_call(kernel, out_shapes, args, scratch=(), micros=10):
    in_vmem = pl.BlockSpec(memory_space=pltpu.VMEM)
    specs = [in_vmem if arg.dtype == jnp.float32 else pl.BlockSpec(memory_space=pltpu.SMEM) for arg in args]
    return pl.pallas_call(
        kernel,
        out_shape=[jax.ShapeDtypeStruct(shape, jnp.float32) for shape in out_shapes],
        in_specs=specs,
        out_specs=[in_vmem] * len(out_shapes),
        scratch_shapes=list(scratch),
        compiler_params=pltpu.CompilerParams(vmem_limit_bytes=24 << 20),
        cost_estimate=pl.CostEstimate(flops=micros * 1000 * 1000 * 1000, bytes_accessed=1 << 20, transcendentals=0),
    )(*args)


def update_kernel(first, shifts, place_ref, old_ref, *refs):
    step = pl.program_id(0)
    rows_refs, refs = refs[:len(shifts)], refs[len(shifts):]
    inverses, refs = refs[:STEPS], refs[STEPS:]
    z_count, _, col_tiles, part, tile = rows_refs[0].shape
    span = z_count // 2
    if first:
        mine_ref, other_ref, new_ref, panels_ref, cols_panel, cols = refs

        @pl.when(step == 0)
        def _():
            def put(slot, rows):
                for k in range(STEPS):
                    for j in range(col_tiles):
                        at = pl.ds(pl.multiple_of(j * tile + slot * part, part), part)
                        cols[at, k * tile:(k + 1) * tile] = rows[k, j]

            place_rows(place_ref, mine_ref, other_ref, put)
            for k in range(STEPS):
                end = (k + 1) * tile
                cols_panel[:, k * tile:end] = product(cols[:, :end], inverses[k][...], ((1,), (1,)))
    else:
        cols_panel, _, _, new_ref, panels_ref = refs

    z_first = span * (step % 2)
    x_count = place_ref[2] // z_count
    z_here = place_ref[1] // x_count
    spots = [lax.rem(z_first + i - z_here + z_count, z_count) for i in range(span)]

    def slices(k, j, i):
        value = rows_refs[0][spots[i], k, j]
        for n in range(1, len(shifts)):
            value = jnp.where(step // 2 == n, rows_refs[n][spots[i], k, j], value)
        return value

    raw = jnp.concatenate(
        [
            jnp.concatenate([slices(k, j, i) for j in range(col_tiles) for i in range(span)], 0)
            for k in range(STEPS)
        ],
        1,
    )
    parts = [product(raw[:, :(k + 1) * tile], inverses[k][...], ((1,), (1,))) for k in range(STEPS)]
    correction = product(jnp.concatenate(parts, 1), cols_panel[...], ((1,), (1,)))
    lane_blocks = tile // LANES
    groups = z_count // 2
    for n in range(col_tiles):
        for i in range(span):
            g, half = divmod(i, 2)
            top = (n * span + i) * part
            tile_row = (n * groups + z_first // 2 + g) * place_ref[3] + place_ref[0]
            for k in range(STEPS):
                panels_ref[n, g, k, half, 0] = jnp.where(tile_row >= k, parts[k][top:top + part], 0.0)
            for j in range(col_tiles):
                keep = jnp.logical_and(tile_row >= STEPS, j * place_ref[2] + place_ref[1] >= STEPS)
                for h in range(lane_blocks):
                    at = pl.ds(j * lane_blocks + h, part, stride=col_tiles * lane_blocks)
                    lo = j * tile + h * LANES
                    fresh = old_ref[n, g, half, 0, at, :] - correction[top:top + part, lo:lo + LANES]
                    new_ref[n, g, half, 0, at, :] = jnp.where(keep, fresh, 0.0)


def update(place, old, rows, shifts, inverses, extra):
    halves, groups, _, x_count, lines, _ = old.shape
    z_count, _, col_tiles, part, tile = rows[0].shape
    depth = STEPS * tile
    first = shifts[0] == 0
    steps = 2 * len(shifts)

    def spot(step, s):
        shift = shifts[0]
        for n in range(1, len(shifts)):
            shift = jnp.where(step // 2 == n, shifts[n], shift)
        return lax.rem(s[1] + shift, x_count)

    whole = pl.BlockSpec(memory_space=pltpu.VMEM)
    old_spec = pl.BlockSpec(
        (halves, groups // 2, 2, 1, lines, LANES), lambda d, s: (0, d % 2, 0, spot(d, s), 0, 0)
    )
    panels_shape = (halves, groups, STEPS, 2, x_count, part, tile)
    panels_spec = pl.BlockSpec(
        (halves, groups // 2, STEPS, 2, 1, part, tile), lambda d, s: (0, d % 2, 0, 0, spot(d, s), 0, 0)
    )
    scratch = []
    out_specs = [old_spec, panels_spec]
    out_shape = [jax.ShapeDtypeStruct(old.shape, jnp.float32), jax.ShapeDtypeStruct(panels_shape, jnp.float32)]
    extra_specs = [whole] * len(extra)
    aliases = {}
    if first:
        scratch = [pltpu.VMEM((col_tiles * tile, depth), jnp.float32)]
        out_specs.append(pl.BlockSpec((col_tiles * tile, depth), lambda d, s: (0, 0)))
        out_shape.append(jax.ShapeDtypeStruct((col_tiles * tile, depth), jnp.float32))
    else:
        extra_specs[1:] = [pl.BlockSpec(memory_space=pl.ANY)] * 2
        at = 2 + len(rows) + STEPS + 1
        aliases = {at: 0, at + 1: 1}
    return pl.pallas_call(
        lambda *refs: update_kernel(first, shifts, *refs),
        grid_spec=pltpu.PrefetchScalarGridSpec(
            num_scalar_prefetch=1,
            grid=(steps,),
            in_specs=[old_spec] + [whole] * (len(rows) + STEPS) + extra_specs,
            out_specs=out_specs,
            scratch_shapes=scratch,
        ),
        out_shape=out_shape,
        input_output_aliases=aliases,
        compiler_params=pltpu.CompilerParams(vmem_limit_bytes=40 << 20),
        cost_estimate=pl.CostEstimate(
            flops=4 * steps * 1000 * 1000 * 1000, bytes_accessed=steps << 20, transcendentals=0
        ),
    )(place, old, *rows, *inverses, *extra)


def in_order(index, parts, wanted):
    count = len(parts)

    def pick(place):
        value = parts[place % count]
        for at in range(1, count):
            value = jnp.where(index == at, parts[(place - at) % count], value)
        return value

    return [pick(place) for place in wanted]


def shards(kernel):
    row_tiles, _, tile, col_tiles, _, _ = kernel.shape
    row_count = lax.axis_size("row")
    col_count = lax.axis_size("col")
    row_index = lax.axis_index("row")
    col_index = lax.axis_index("col")
    x_count = 4
    y_count = row_count // 2
    z_count = col_count // x_count
    col, row = grid_perms(row_count, z_count, x_count)
    depth = STEPS * tile
    part = tile // row_count
    groups = col_count // row_count
    place = jnp.stack([row_index, col_index, jnp.int32(col_count), jnp.int32(row_count)]).astype(jnp.int32)

    def from_z(value, k):
        return lax.ppermute(value, "col", col(lambda z, x: (z - k, x)))

    def from_x(value, k):
        return lax.ppermute(value, "col", col(lambda z, x: (z, x - k)))

    def from_y(value, k):
        return lax.ppermute(value, "row", row(lambda y, core: (y - k, core)))

    top = kernel[0].reshape(tile, col_tiles, row_count, part).transpose(2, 1, 3, 0)
    piece = lax.all_to_all(top, "row", 0, 0, tiled=True)[:STEPS]

    cross = []
    for r in range(row_count):
        for c in range(col_count):
            g, c8 = divmod(c, row_count)
            cross.append((r * col_count + c, c8 * col_count + g * row_count + r))

    z = col_index // x_count
    x = col_index % x_count

    def from_rows(value):
        return [value] + [from_y(value, k) for k in range(1, y_count)]

    def from_core(value):
        return lax.ppermute(value, "row", row(lambda y, core: (y, 1 - core)))

    def spread(value, level):
        moved = lax.ppermute(
            value, "col", col(lambda z, x: (z + level, x), lambda z, x: z % (2 * level) == 0 and x < STEPS)
        )
        return value + moved

    stage = lax.optimization_barrier
    swapped = lax.ppermute(piece, ("row", "col"), cross)
    corner = jnp.where(z == 0, piece[:, 0], 0.0)
    level = z_count // 2
    while level > 1:
        corner = spread(corner, level)
        level //= 2
    corner, swapped, piece = stage((corner, swapped, piece))

    ups, downs = [swapped], [swapped]

    def relay():
        ups.append(from_z(ups[-1], -1))
        downs.append(from_z(downs[-1], 1))

    corner = spread(corner, level)
    relay()
    cols = from_rows(piece)
    corner, ups[-1], downs[-1] = stage((corner, ups[-1], downs[-1]))

    corner = [corner] + [from_x(corner, k) for k in range(1, x_count)]
    relay()
    corner, ups[-1], downs[-1], cols = stage((corner, ups[-1], downs[-1], cols))
    cols = jnp.stack(cols)
    cols = [cols, from_core(cols)]

    corner = in_order(x, corner, range(STEPS))
    tiles = from_rows(jnp.stack([corner[i][k] for k in range(STEPS) for i in range(k, STEPS)]))
    relay()
    tiles, ups[-1], downs[-1] = stage((tiles, ups[-1], downs[-1]))

    mine = jnp.stack(tiles)
    other = from_core(mine)
    far = jnp.concatenate([from_z(ups[-1][:, :1], -1), from_z(downs[-1][:, 1:], 1)], 1)
    here = jnp.stack(downs + [far] + ups[:0:-1])
    other, here, cols = stage((other, here, cols))

    right, left = from_x(here, 1), from_x(here, -1)
    square = (tile, tile)
    x0, low0, rest = local_call(
        first_factor,
        [square, (2 * tile, tile), (3 * tile, tile)],
        (place, mine, other),
        [pltpu.VMEM((tiles[0].shape[0] * tile, tile), jnp.float32)],
    )
    x1, low1, last = local_call(second_factor, [(tile, 2 * tile), square, square], (rest, x0, low0))
    x2, = local_call(third_factor, [(tile, depth)], (last, x0, low0, x1, low1))
    x2, right, left = stage((x2, right, left))
    across = jnp.concatenate([from_x(right[:z_count // 2], 1), from_x(left[z_count // 2:], -1)])
    old = kernel.reshape(col_tiles, groups, 2, x_count, part * col_tiles * tile // LANES, LANES)
    inverses = (x0, x1, x2)
    trailing, panels, cols_panel = update(place, old, [here], (0,), inverses, cols)
    trailing, panels = update(place, old, [right, left], (1, x_count - 1), inverses, (cols_panel, trailing, panels))
    trailing, panels = update(place, old, [across], (2,), inverses, (cols_panel, trailing, panels))
    panels = panels.reshape(row_tiles, STEPS, tile, tile).transpose(0, 2, 1, 3).reshape(row_tiles, 1, tile, STEPS, tile)
    return (trailing.reshape(kernel.shape), panels)


def solution(mesh):
    in_specs = (P(None, "row", None, None, "col", None),)
    out_specs = (P(None, "row", None, None, "col", None), P(None, "row", None, None, None))
    return jax.shard_map(shards, mesh=mesh, in_specs=in_specs, out_specs=out_specs, check_vma=False)
```

```python
import jax
import jax.numpy as jnp
from jax import lax
from jax.experimental import pallas as pl
from jax.experimental.pallas import tpu as pltpu
from jax.sharding import PartitionSpec as P

STEPS = 3
LANES = 128
SUBLANES = 8
HIGHEST = lax.Precision.HIGHEST


def grid_perms(row_count, z_count, x_count):
    def col(move, keep=lambda z, x: True):
        pairs = []
        for z in range(z_count):
            for x in range(x_count):
                if keep(z, x):
                    z2, x2 = move(z, x)
                    pairs.append((z * x_count + x, (z2 % z_count) * x_count + x2 % x_count))
        return pairs

    def row(move):
        pairs = []
        for y in range(row_count // 2):
            for core in range(2):
                y2, core2 = move(y, core)
                pairs.append((y * 2 + core, (y2 % (row_count // 2)) * 2 + core2))
        return pairs

    return col, row


def product(a, b, dims):
    return lax.dot_general(a, b, (dims, ((), ())), precision=HIGHEST, preferred_element_type=jnp.float32)


def from_lane(v, lane):
    return jnp.broadcast_to(v[:, lane:lane + 1], (SUBLANES, LANES))


def from_row(v, row):
    return jnp.broadcast_to(v[row:row + 1, :], (SUBLANES, LANES))


def eliminate(t):
    count = len(t)
    rows = lax.broadcasted_iota(jnp.int32, (SUBLANES, LANES), 0)
    lanes = lax.broadcasted_iota(jnp.int32, (SUBLANES, LANES), 1)
    r = [jnp.where(lanes == rows + SUBLANES * k, jnp.float32(1.0), jnp.float32(0.0)) for k in range(count)]
    t = list(t)
    out = []
    for j in range(count):
        tj, rj = t[j], r[j]
        c = [from_lane(tj, SUBLANES * j + m) for m in range(SUBLANES)]
        e = {}
        inverse_pivots = []
        pivots = jnp.ones((SUBLANES, LANES), jnp.float32)
        for i in range(SUBLANES):
            d = from_row(c[i], i)
            pivots = jnp.where(rows == i, d, pivots)
            inverse_pivots.append(1.0 / d)
            f = jnp.where(rows > i, c[i] * inverse_pivots[i], 0.0)
            for m in range(i + 1, SUBLANES):
                e[i, m] = from_row(c[m], i)
                c[m] = c[m] - f * e[i, m]
            tj = tj - f * from_row(tj, i)
            rj = rj - f * from_row(rj, i)
        out.append(rj * lax.rsqrt(pivots))
        if j + 1 == count:
            break
        tb = [from_row(tj, i) for i in range(SUBLANES)]
        rb = [from_row(rj, i) for i in range(SUBLANES)]
        for k in range(j + 1, count):
            c = [from_lane(t[k], SUBLANES * j + m) for m in range(SUBLANES)]
            for i in range(SUBLANES):
                f = c[i] * inverse_pivots[i]
                for m in range(i + 1, SUBLANES):
                    c[m] = c[m] - f * e[i, m]
                t[k] = t[k] - f * tb[i]
                r[k] = r[k] - f * rb[i]
    return jnp.concatenate(out, 0)


def place_rows(place_ref, mine_ref, other_ref, put):
    y_count = mine_ref.shape[0]
    y = place_ref[0] // 2
    core = place_ref[0] % 2
    for k in range(y_count):
        first = 2 * lax.rem(y + k, y_count)
        put(first + core, mine_ref[k])
        put(first + 1 - core, other_ref[k])


def factor_columns(column):
    size = LANES

    def inverse(block):
        return eliminate([block[k:k + SUBLANES] for k in range(0, size, SUBLANES)])

    left, right = column[:, :size], column[size:, size:]
    first = inverse(left[:size])
    low = product(left[size:], first, ((1,), (1,)))
    right = right - product(low, low[:size], ((1,), (1,)))
    second = inverse(right[:size])
    corner = -product(second, product(low[:size], first, ((1,), (0,))), ((1,), (0,)))
    inverse_factor = jnp.concatenate(
        [jnp.concatenate([first, jnp.zeros((size, size), jnp.float32)], 1), jnp.concatenate([corner, second], 1)], 0
    )
    if right.shape[0] == size:
        return inverse_factor, None
    return inverse_factor, jnp.concatenate([low[size:], product(right[size:], second, ((1,), (1,)))], 1)


def factor_kernel(place_ref, mine_ref, other_ref, x0_ref, x1_ref, x2_ref, corner):
    tiles, part = mine_ref.shape[1:3]
    tile = x0_ref.shape[0]

    def put(slot, rows):
        for i in range(tiles):
            corner[pl.ds(pl.multiple_of(i * tile + slot * part, part), part), :] = rows[i]

    place_rows(place_ref, mine_ref, other_ref, put)
    x0, low0 = factor_columns(corner[:3 * tile])
    x0_ref[...] = x0
    x1, low1 = factor_columns(corner[3 * tile:5 * tile] - product(low0, low0[:tile], ((1,), (1,))))
    rest = corner[5 * tile:] - product(low0[tile:], low0[tile:], ((1,), (1,)))
    x2, _ = factor_columns(rest - product(low1, low1, ((1,), (1,))))
    before = product(low0, x0, ((1,), (0,)))
    row1 = jnp.concatenate([-product(x1, before[:tile], ((1,), (0,))), x1], 1)
    x1_ref[...] = row1
    past = product(low1, row1, ((1,), (0,)))
    x2_ref[:, :tile] = -product(x2, before[tile:] + past[:, :tile], ((1,), (0,)))
    x2_ref[:, tile:2 * tile] = -product(x2, past[:, tile:], ((1,), (0,)))
    x2_ref[:, 2 * tile:] = x2


def local_call(kernel, out_shapes, args, scratch=(), micros=30):
    in_vmem = pl.BlockSpec(memory_space=pltpu.VMEM)
    specs = [pl.BlockSpec(memory_space=pltpu.SMEM)] + [in_vmem] * (len(args) - 1)
    return pl.pallas_call(
        kernel,
        out_shape=[jax.ShapeDtypeStruct(shape, jnp.float32) for shape in out_shapes],
        in_specs=specs,
        out_specs=[in_vmem] * len(out_shapes),
        scratch_shapes=list(scratch),
        compiler_params=pltpu.CompilerParams(vmem_limit_bytes=32 << 20),
        cost_estimate=pl.CostEstimate(flops=micros * 1000 * 1000 * 1000, bytes_accessed=1 << 20, transcendentals=0),
    )(*args)


def update_kernel(first, shifts, place_ref, old_ref, *refs):
    step = pl.program_id(0)
    rows_refs, refs = refs[:len(shifts)], refs[len(shifts):]
    inverses, refs = refs[:STEPS], refs[STEPS:]
    z_count, _, col_tiles, part, tile = rows_refs[0].shape
    span = z_count // 2
    if first:
        mine_ref, other_ref, new_ref, panels_ref, cols_panel, cols = refs

        @pl.when(step == 0)
        def _():
            def put(slot, rows):
                for k in range(STEPS):
                    for j in range(col_tiles):
                        at = pl.ds(pl.multiple_of(j * tile + slot * part, part), part)
                        cols[at, k * tile:(k + 1) * tile] = rows[k, j]

            place_rows(place_ref, mine_ref, other_ref, put)
            for k in range(STEPS):
                end = (k + 1) * tile
                cols_panel[:, k * tile:end] = product(cols[:, :end], inverses[k][...], ((1,), (1,)))
    else:
        cols_panel, _, _, new_ref, panels_ref = refs

    z_first = span * (step % 2)
    x_count = place_ref[2] // z_count
    z_here = place_ref[1] // x_count
    spots = [lax.rem(z_first + i - z_here + z_count, z_count) for i in range(span)]

    def slices(k, j, i):
        value = rows_refs[0][spots[i], k, j]
        for n in range(1, len(shifts)):
            value = jnp.where(step // 2 == n, rows_refs[n][spots[i], k, j], value)
        return value

    raw = jnp.concatenate(
        [
            jnp.concatenate([slices(k, j, i) for j in range(col_tiles) for i in range(span)], 0)
            for k in range(STEPS)
        ],
        1,
    )
    parts = [product(raw[:, :(k + 1) * tile], inverses[k][...], ((1,), (1,))) for k in range(STEPS)]
    correction = product(jnp.concatenate(parts, 1), cols_panel[...], ((1,), (1,)))
    lane_blocks = tile // LANES
    groups = z_count // 2
    for n in range(col_tiles):
        for i in range(span):
            g, half = divmod(i, 2)
            top = (n * span + i) * part
            tile_row = (n * groups + z_first // 2 + g) * place_ref[3] + place_ref[0]
            for k in range(STEPS):
                panels_ref[n, g, k, half, 0] = jnp.where(tile_row >= k, parts[k][top:top + part], 0.0)
            for j in range(col_tiles):
                keep = jnp.logical_and(tile_row >= STEPS, j * place_ref[2] + place_ref[1] >= STEPS)
                for h in range(lane_blocks):
                    at = pl.ds(j * lane_blocks + h, part, stride=col_tiles * lane_blocks)
                    lo = j * tile + h * LANES
                    fresh = old_ref[n, g, half, 0, at, :] - correction[top:top + part, lo:lo + LANES]
                    new_ref[n, g, half, 0, at, :] = jnp.where(keep, fresh, 0.0)


def update(place, old, rows, shifts, inverses, extra):
    halves, groups, _, x_count, lines, _ = old.shape
    z_count, _, col_tiles, part, tile = rows[0].shape
    depth = STEPS * tile
    first = shifts[0] == 0
    steps = 2 * len(shifts)

    def spot(step, s):
        shift = shifts[0]
        for n in range(1, len(shifts)):
            shift = jnp.where(step // 2 == n, shifts[n], shift)
        return lax.rem(s[1] + shift, x_count)

    whole = pl.BlockSpec(memory_space=pltpu.VMEM)
    old_spec = pl.BlockSpec(
        (halves, groups // 2, 2, 1, lines, LANES), lambda d, s: (0, d % 2, 0, spot(d, s), 0, 0)
    )
    panels_shape = (halves, groups, STEPS, 2, x_count, part, tile)
    panels_spec = pl.BlockSpec(
        (halves, groups // 2, STEPS, 2, 1, part, tile), lambda d, s: (0, d % 2, 0, 0, spot(d, s), 0, 0)
    )
    scratch = []
    out_specs = [old_spec, panels_spec]
    out_shape = [jax.ShapeDtypeStruct(old.shape, jnp.float32), jax.ShapeDtypeStruct(panels_shape, jnp.float32)]
    extra_specs = [whole] * len(extra)
    aliases = {}
    if first:
        scratch = [pltpu.VMEM((col_tiles * tile, depth), jnp.float32)]
        out_specs.append(pl.BlockSpec((col_tiles * tile, depth), lambda d, s: (0, 0)))
        out_shape.append(jax.ShapeDtypeStruct((col_tiles * tile, depth), jnp.float32))
    else:
        extra_specs[1:] = [pl.BlockSpec(memory_space=pl.ANY)] * 2
        at = 2 + len(rows) + STEPS + 1
        aliases = {at: 0, at + 1: 1}
    return pl.pallas_call(
        lambda *refs: update_kernel(first, shifts, *refs),
        grid_spec=pltpu.PrefetchScalarGridSpec(
            num_scalar_prefetch=1,
            grid=(steps,),
            in_specs=[old_spec] + [whole] * (len(rows) + STEPS) + extra_specs,
            out_specs=out_specs,
            scratch_shapes=scratch,
        ),
        out_shape=out_shape,
        input_output_aliases=aliases,
        compiler_params=pltpu.CompilerParams(vmem_limit_bytes=40 << 20),
        cost_estimate=pl.CostEstimate(
            flops=4 * steps * 1000 * 1000 * 1000, bytes_accessed=steps << 20, transcendentals=0
        ),
    )(place, old, *rows, *inverses, *extra)


def in_order(index, parts, wanted):
    count = len(parts)

    def pick(place):
        value = parts[place % count]
        for at in range(1, count):
            value = jnp.where(index == at, parts[(place - at) % count], value)
        return value

    return [pick(place) for place in wanted]


def shards(kernel):
    row_tiles, _, tile, col_tiles, _, _ = kernel.shape
    row_count = lax.axis_size("row")
    col_count = lax.axis_size("col")
    row_index = lax.axis_index("row")
    col_index = lax.axis_index("col")
    x_count = 4
    y_count = row_count // 2
    z_count = col_count // x_count
    col, row = grid_perms(row_count, z_count, x_count)
    depth = STEPS * tile
    part = tile // row_count
    groups = col_count // row_count
    place = jnp.stack([row_index, col_index, jnp.int32(col_count), jnp.int32(row_count)]).astype(jnp.int32)

    def from_z(value, k):
        return lax.ppermute(value, "col", col(lambda z, x: (z - k, x)))

    def from_x(value, k):
        return lax.ppermute(value, "col", col(lambda z, x: (z, x - k)))

    def from_y(value, k):
        return lax.ppermute(value, "row", row(lambda y, core: (y - k, core)))

    def over_rows(value):
        mine = jnp.stack([value] + [from_y(value, k) for k in range(1, y_count)])
        return mine, lax.ppermute(mine, "row", row(lambda y, core: (y, 1 - core)))

    top = kernel[0].reshape(tile, col_tiles, row_count, part).transpose(2, 1, 3, 0)
    piece = lax.all_to_all(top, "row", 0, 0, tiled=True)[:STEPS]

    cross = []
    for r in range(row_count):
        for c in range(col_count):
            g, c8 = divmod(c, row_count)
            cross.append((r * col_count + c, c8 * col_count + g * row_count + r))

    z = col_index // x_count
    x = col_index % x_count
    swapped = lax.ppermute(piece, ("row", "col"), cross)
    corner = jnp.where(z == 0, piece[:, 0], 0.0)
    level = z_count // 2
    while level:
        corner = corner + lax.ppermute(
            corner, "col", col(lambda z, x: (z + level, x), lambda z, x: z % (2 * level) == 0 and x < STEPS)
        )
        level //= 2
    corner, swapped = lax.optimization_barrier((corner, swapped))
    corner = in_order(x, [corner] + [from_x(corner, k) for k in range(1, x_count)], range(STEPS))
    tiles = jnp.stack([corner[i][k] for k in range(STEPS) for i in range(k, STEPS)])
    mine, other = over_rows(tiles)

    ups, downs = [swapped], [swapped]
    for k in range(1, z_count // 2):
        ups.append(from_z(ups[-1], -1))
        downs.append(from_z(downs[-1], 1))
    far = jnp.concatenate([from_z(ups[-1][:, :1], -1), from_z(downs[-1][:, 1:], 1)], 1)
    here = jnp.stack(downs + [far] + ups[:0:-1])

    cols = over_rows(piece)
    other, here = lax.optimization_barrier((other, here))
    right, left = from_x(here, 1), from_x(here, -1)
    x0, x1, x2 = local_call(
        factor_kernel,
        [(tile, (k + 1) * tile) for k in range(STEPS)],
        (place, mine, other),
        [pltpu.VMEM((tiles.shape[0] * tile, tile), jnp.float32)],
    )

    x0, right, left = lax.optimization_barrier((x0, right, left))
    across = jnp.concatenate([from_x(right[:z_count // 2], 1), from_x(left[z_count // 2:], -1)])
    old = kernel.reshape(col_tiles, groups, 2, x_count, part * col_tiles * tile // LANES, LANES)
    inverses = (x0, x1, x2)
    trailing, panels, cols_panel = update(place, old, [here], (0,), inverses, cols)
    trailing, panels = update(place, old, [right, left], (1, x_count - 1), inverses, (cols_panel, trailing, panels))
    trailing, panels = update(place, old, [across], (2,), inverses, (cols_panel, trailing, panels))
    panels = panels.reshape(row_tiles, STEPS, tile, tile).transpose(0, 2, 1, 3).reshape(row_tiles, 1, tile, STEPS, tile)
    return (trailing.reshape(kernel.shape), panels)


def solution(mesh):
    in_specs = (P(None, "row", None, None, "col", None),)
    out_specs = (P(None, "row", None, None, "col", None), P(None, "row", None, None, None))
    return jax.shard_map(shards, mesh=mesh, in_specs=in_specs, out_specs=out_specs, check_vma=False)
```
